32 devices in a mesh: clip: 2 (over y), xt: 4 (over z), tb: 2 (over x), luma: 2 (over core).
Axes of the slice: x: 2, y: 2, z: 4, core: 2. Of those that a mesh axis runs over, the one named last changes fastest.
Arguments:
- target: float32 [8, 2, 2, 4, 8, 8, 2, 128], P(('clip', 'xt'), 'tb', 'luma'), parts along dimension 0, may hold values from -1 to 6
- confidence: float32 [8, 2, 2, 4, 8, 8, 2, 128], P(('clip', 'xt'), 'tb', 'luma'), parts along dimension 0, may hold values from 0.05 to 1
- normalizer: float32 [8, 2, 2, 4, 8, 8, 2, 128], P(('clip', 'xt'), 'tb', 'luma'), parts along dimension 0, may hold values from 0.5 to 1
- brick_slots: int32 [8, 2, 2, 4], P(('clip', 'xt'), 'tb', 'luma'), parts along dimension 0, may hold values from 0 to 7, as said below
- brick_counts: int32 [8, 2, 2], P(('clip', 'xt'), 'tb', 'luma'), parts along dimension 0, may hold values from 1 to 4, as said below
Outputs:
- solution: float32 [8, 2, 2, 4, 8, 8, 2, 128], P(('clip', 'xt'), 'tb', 'luma'), parts along dimension 0
The draws below stay inside these ranges and needn't reach their ends.
There are 2 independent parts, one for each index of `clip`. The reference program is written for one: setup_inputs(seed, part) draws one part's arguments, and reference() takes and returns one part's arrays. A program takes and returns all parts, laid end to end along the dimension named above; each array names one. Nothing has to cross between parts.
Inputs may be any that keep to these rules, and one draw needn't show every extreme that they name: `brick_slots`: in each device's list the 4 entries name different positions; position s is the brick (s // 4, (s // 2) % 2, s % 2) of the device's 2 x 2 x 2 region of time, luma and x bricks. The first brick_counts entries of a device's list are its occupied bricks; some device has 4.
All inputs are finite; a program needn't handle non-finite values.
Results may differ from the reference program's by a relative error of at most 0.0003.
Values sent between devices are 32-bit elements; how exact they have to be, the bound alone decides.
A program may use at most 64 MiB of HBM per device.

```python
import math
import jax
import jax.numpy as jnp
from jax import lax

BT = 8
BL = 8
BX = 2
YC = 128
RT = 2
RL = 2
RX = 2
MAXB = 4
ITERS = 3
SLOTS = 8
NT = 32
NL = 32
NX = 16
N_XT = 4
N_TB = 2
N_LUMA = 2


def draw_target(key, part):
    key = jax.random.fold_in(key, 13)
    shape = (N_XT, N_TB, N_LUMA, MAXB, BT, BL, BX, YC)
    values = jnp.clip(3.0 + jax.random.normal(key, shape, jnp.float32), -1.0, 6.0)
    return values.astype(jnp.float32)


def draw_brick_counts(key, part):
    key = jax.random.fold_in(key, 11)
    first_key, second_key = jax.random.split(key)
    devices_all = N_XT * N_TB * N_LUMA
    counts = jax.random.randint(first_key, (devices_all,), 1, MAXB + 1, dtype=jnp.int32)
    chosen = jax.random.randint(second_key, (), 0, devices_all, dtype=jnp.int32)
    counts = counts.at[chosen].set(MAXB)
    return counts.reshape(N_XT, N_TB, N_LUMA).astype(jnp.int32)


def draw_brick_slots(key, part):
    key = jax.random.fold_in(key, 12)
    devices_all = N_XT * N_TB * N_LUMA
    keys = jax.random.split(key, devices_all)
    orders = jax.vmap(lambda single: jax.random.permutation(single, SLOTS))(keys)
    return orders[:, :MAXB].reshape(N_XT, N_TB, N_LUMA, MAXB).astype(jnp.int32)


def block_scale(rng, dims, pieces, least, largest):
    def one(position, shards_of):
        heights = jax.random.uniform(jax.random.fold_in(jax.random.fold_in(rng, 6), position), (shards_of,), jnp.float32, least / len(pieces), largest / len(pieces))
        return jnp.repeat(jnp.exp(heights), dims[position] // shards_of).reshape((-1,) + (1,) * (len(dims) - position - 1))

    level = one(*pieces[0])
    for cut in pieces[1:]:
        level = level * one(*cut)
    return level


def setup_inputs(seed: int = 0, part: int = 0) -> dict:
    splits = jax.random.split(jax.random.key(seed), 6)
    part_splits = jax.random.split(jax.random.fold_in(splits[5], part), 6)
    return {
        "target": draw_target(jax.random.fold_in(jax.random.fold_in(splits[5], part), 71), part),
        "confidence": jnp.clip(jnp.exp(math.log(1.0) - 2.9957323 * jax.random.uniform(part_splits[1], (N_XT, N_TB, N_LUMA, MAXB, BT, BL, BX, YC), jnp.float32) ** block_scale(part_splits[1], (N_XT, N_TB, N_LUMA, MAXB, BT, BL, BX, YC), ((0, 4), (1, 2), (2, 2)), -0.2, 0.2)), 0.05, 1.0),
        "normalizer": jnp.clip(0.5 + 0.5 * jax.random.uniform(part_splits[2], (N_XT, N_TB, N_LUMA, MAXB, BT, BL, BX, YC), jnp.float32) ** block_scale(part_splits[2], (N_XT, N_TB, N_LUMA, MAXB, BT, BL, BX, YC), ((0, 4), (1, 2), (2, 2)), -0.2, 0.2), 0.5, 1.0),
        "brick_slots": draw_brick_slots(jax.random.fold_in(jax.random.fold_in(splits[5], part), 71), part),
        "brick_counts": draw_brick_counts(jax.random.fold_in(jax.random.fold_in(splits[5], part), 71), part),
    }


smoothness = 8.0


def to_grid(compact, brick_slots, brick_counts):
    occupied = jnp.arange(MAXB, dtype=jnp.int32)[None, None, None, :] < brick_counts[..., None]
    places = jnp.where(occupied, brick_slots, SLOTS).astype(jnp.int32)
    flat = compact.reshape(-1, MAXB, BT, BL, BX, YC)
    where_to = places.reshape(-1, MAXB)

    def place_one(pair):
        values, targets = pair
        region = jnp.zeros((SLOTS + 1, BT, BL, BX, YC), compact.dtype).at[targets].set(values)
        return region[:SLOTS]

    regions = lax.map(place_one, (flat, where_to))
    regions = regions.reshape(N_XT, N_TB, N_LUMA, RT, RL, RX, BT, BL, BX, YC)
    regions = regions.transpose(1, 3, 6, 2, 4, 7, 0, 5, 8, 9)
    return regions.reshape(NT, NL, NX, YC)


def from_grid(grid, brick_slots, brick_counts):
    regions = grid.reshape(N_TB, RT, BT, N_LUMA, RL, BL, N_XT, RX, BX, YC)
    regions = regions.transpose(6, 0, 3, 1, 4, 7, 2, 5, 8, 9).reshape(-1, SLOTS, BT, BL, BX, YC)
    occupied = jnp.arange(MAXB, dtype=jnp.int32)[None, None, None, :] < brick_counts[..., None]
    places = jnp.where(occupied, brick_slots, 0).astype(jnp.int32).reshape(-1, MAXB)
    weights = occupied.astype(grid.dtype).reshape(-1, MAXB)

    def take_one(triple):
        region, targets, keep = triple
        return region[targets] * keep[:, None, None, None, None]

    picked = lax.map(take_one, (regions, places, weights))
    return picked.reshape(N_XT, N_TB, N_LUMA, MAXB, BT, BL, BX, YC)


def smooth_axis(padded, axis):
    length = padded.shape[axis]
    first = lax.slice_in_dim(padded, 0, length - 2, axis=axis)
    middle = lax.slice_in_dim(padded, 1, length - 1, axis=axis)
    last = lax.slice_in_dim(padded, 2, length, axis=axis)
    return 0.25 * first + 0.5 * middle + 0.25 * last


def smooth(values):
    padded = jnp.pad(values, ((1, 1), (1, 1), (1, 1), (0, 0)))
    padded = smooth_axis(padded, 0)
    padded = smooth_axis(padded, 1)
    padded = smooth_axis(padded, 2)
    padded = jnp.pad(padded, ((0, 0), (0, 0), (0, 0), (1, 1)))
    return smooth_axis(padded, 3)


def reference(target, confidence, normalizer, brick_slots, brick_counts):
    occupied = to_grid(jnp.ones_like(target), brick_slots, brick_counts)
    tgrid = to_grid(target, brick_slots, brick_counts)
    cgrid = to_grid(confidence, brick_slots, brick_counts)
    ngrid = to_grid(normalizer, brick_slots, brick_counts)
    diagonal = smoothness * ngrid * smooth(ngrid) + cgrid
    inverse = occupied / jnp.where(occupied > 0, diagonal, 1.0)

    def operator_apply(values):
        return diagonal * values - smoothness * ngrid * smooth(ngrid * values)

    residual = cgrid * tgrid
    sol = jnp.zeros_like(residual)
    precond_r = inverse * residual
    image_u = operator_apply(precond_r)
    for iteration in range(ITERS):
        gamma = jnp.sum(residual * precond_r)
        delta = jnp.sum(image_u * precond_r)
        if iteration == 0:
            alpha = gamma / delta
            direction = precond_r
        else:
            beta = gamma / gamma_prev
            alpha = gamma / (delta - beta * gamma / alpha_prev)
            direction = precond_r + beta * direction
        sol = sol + alpha * direction
        if iteration + 1 < ITERS:
            precond_w = inverse * image_u
            image_pw = operator_apply(precond_w)
            if iteration == 0:
                image_pdir = image_pw
                precond_dir = precond_w
                image_dir = image_u
            else:
                image_pdir = image_pw + beta * image_pdir
                precond_dir = precond_w + beta * precond_dir
                image_dir = image_u + beta * image_dir
            residual = residual - alpha * image_dir
            precond_r = precond_r - alpha * precond_dir
            image_u = image_u - alpha * image_pdir
        gamma_prev = gamma
        alpha_prev = alpha
    return from_grid(sol, brick_slots, brick_counts)
```

```python
import functools

import jax
import jax.numpy as jnp
from jax import lax
from jax.experimental import pallas as pl
from jax.experimental.pallas import tpu as pltpu
from jax.sharding import PartitionSpec as P

MESH = pl.DeviceIdType.MESH
SHIFT = 0.5
STAGES = 4
SIDES = (-1, 0, 1)
MESSAGES = [(dx, dt, dl) for dl in (0, 1) for dx in SIDES for dt in SIDES if (dx, dt, dl) != (0, 0, 0)]
NEAR = [m for m in MESSAGES if m[0] == 0]
FAR = [m for m in MESSAGES if m[0] != 0]


def kernel(
    nx, nt,
    slots, counts, target, confidence, normalizer, out,
    tin, cin, nin, bricks, n_, c_, r_, d_, m_, p0_, p1_, p2_, u0_,
    q_, es, er, fs, ff, acc, gathered,
    in_sem, send_sem, recv_sem, sum_send, sum_recv,
):
    ix, it, il = lax.axis_index("xt"), lax.axis_index("tb"), lax.axis_index("luma")
    peers = nx * nt * 2
    me = (ix * nt + it) * 2 + il

    loads = [
        pltpu.make_async_copy(src, dst, in_sem.at[i])
        for i, (src, dst) in enumerate(((normalizer, nin), (confidence, cin), (target, tin)))
    ]
    for load in loads:
        load.start()

    @pl.when(ix == 0)
    def _():
        q_[:, 0] = jnp.zeros_like(q_[:, 0])
        er[:, 0] = jnp.zeros_like(er[:, 0])

    @pl.when(ix == nx - 1)
    def _():
        q_[:, 5] = jnp.zeros_like(q_[:, 5])
        er[:, 5] = jnp.zeros_like(er[:, 5])

    @pl.when(it == 0)
    def _():
        q_[:, :, 0] = jnp.zeros_like(q_[:, :, 0])
        er[:, :, 0:8] = jnp.zeros_like(er[:, :, 0:8])

    @pl.when(it == nt - 1)
    def _():
        q_[:, :, 17] = jnp.zeros_like(q_[:, :, 17])
        er[:, :, 24:32] = jnp.zeros_like(er[:, :, 24:32])

    def peer_id(r):
        other = lax.rem(me + r, peers)
        return {"xt": lax.div(other, 2 * nt), "tb": lax.rem(lax.div(other, 2), nt), "luma": lax.rem(other, 2)}

    def each_peer(act):
        if peers <= 16:
            for r in range(1, peers):
                act(r)
        else:
            def step(r, carry):
                act(r)
                return carry
            lax.fori_loop(1, peers, step, 0)

    barrier = pltpu.get_barrier_semaphore()
    each_peer(lambda r: pl.semaphore_signal(barrier, inc=1, device_id=peer_id(r), device_id_type=MESH))

    row = lax.broadcasted_iota(jnp.int32, (16, 128), 0)
    col = lax.broadcasted_iota(jnp.int32, (16, 128), 1)
    edge = jnp.where(row == jnp.where(il == 0, 15, 0), 1.0, 0.0).astype(jnp.float32)
    zero = jnp.zeros((16, 128), jnp.float32)

    entry, here = [], []
    for s in range(8):
        k_s, h_s = jnp.int32(0), jnp.float32(0.0)
        for k in range(4):
            hit = jnp.logical_and(slots[0, 0, 0, k] == s, k < counts[0, 0, 0])
            k_s = jnp.where(hit, k, k_s)
            h_s = jnp.where(hit, 1.0, h_s)
        entry.append(k_s)
        here.append(h_s)

    def place(source, body):
        def step(i, carry):
            for s in range(8):
                bricks[s, i] = source[entry[s], i] * here[s]
            for s in range(8):
                rt, rl, rx = s // 4, (s // 2) % 2, s % 2
                for lx in range(2):
                    values = bricks[s, i, pl.ds(lx, 8, stride=2), :]
                    body(values, (rx * 2 + lx, rt * 8 + i, pl.ds(rl * 8, 8)))
            return carry
        lax.fori_loop(0, 8, step, 0)

    def emit(stage, x, t, values):
        tile = (
            2.0 * values
            + jnp.where(col == 0, 0.0, pltpu.roll(values, 1, 1))
            + jnp.where(col == 127, 0.0, pltpu.roll(values, 127, 1))
        )
        q_[stage, x + 1, t + 1] = tile
        es[stage, x, pl.ds(t, 1), :] = jnp.where(il == 0, tile[15:16], tile[0:1])

    def message(stage, which):
        dx, dt, dl = which
        i = MESSAGES.index(which)
        to = {"xt": ix + dx, "tb": it + dt, "luma": 1 - il if dl else il}
        if dl == 0:
            xs = {1: (4, 0), -1: (1, 5), 0: (pl.ds(1, 4), pl.ds(1, 4))}[dx]
            ts = {1: (16, 0), -1: (1, 17), 0: (pl.ds(1, 16), pl.ds(1, 16))}[dt]
            src, dst = (q_.at[stage, xs[j], ts[j]] for j in (0, 1))
        else:
            xs = {1: (3, 0), -1: (0, 5), 0: (pl.ds(0, 4), pl.ds(1, 4))}[dx]
            ts = {
                1: (pl.ds(8, 8), pl.ds(0, 8)),
                -1: (pl.ds(0, 8), pl.ds(24, 8)),
                0: (pl.ds(0, 16), pl.ds(8, 16)),
            }[dt]
            src, dst = es.at[stage, xs[0], ts[0]], er.at[stage, xs[1], ts[1]]
        return pltpu.make_async_remote_copy(
            src_ref=src, dst_ref=dst, send_sem=send_sem.at[stage, i], recv_sem=recv_sem.at[stage, i],
            device_id=to, device_id_type=MESH,
        )

    def guarded(which, sign, act):
        dx, dt, _ = which
        conds = []
        for d, at, size in ((dx * sign, ix, nx), (dt * sign, it, nt)):
            if d == 1:
                conds.append(at < size - 1)
            elif d == -1:
                conds.append(at > 0)
        if conds:
            pl.when(functools.reduce(jnp.logical_and, conds))(act)
        else:
            act()

    def send(stage, group):
        for which in group:
            guarded(which, 1, lambda which=which: message(stage, which).start())

    def receive(stage, group):
        for which in group:
            guarded(which, -1, lambda which=which: message(stage, which).wait_recv())

    def spread(stage, xs, update, carry):
        for x in xs:
            g = er[stage, x] + 2.0 * er[stage, x + 1] + er[stage, x + 2]
            fs[x] = g
            ff[x] = fs[x, pl.ds(7, 16)] + 2.0 * fs[x, pl.ds(8, 16)] + fs[x, pl.ds(9, 16)]
        need = sorted({x + d for x in xs for d in (0, 1, 2)})

        def step(t, carry):
            sums = {
                x: q_[stage, x, t] + 2.0 * q_[stage, x, t + 1] + q_[stage, x, t + 2] for x in need
            }
            for x in xs:
                a = sums[x] + 2.0 * sums[x + 1] + sums[x + 2]
                smoothed = (
                    2.0 * a
                    + jnp.where(row == 0, 0.0, pltpu.roll(a, 1, 0))
                    + jnp.where(row == 15, 0.0, pltpu.roll(a, 15, 0))
                    + edge * ff[x, pl.ds(t, 1), :]
                )
                carry = update(x, t, smoothed, carry)
            return carry

        return lax.fori_loop(0, 16, step, carry)

    def keep_sum(i, total):
        acc[pl.ds(i, 1), :] = jnp.sum(total, axis=0, keepdims=True)

    loads[0].wait()

    def put_n(values, at):
        n_[at] = values

    place(nin, put_n)

    def first(t, carry):
        for x in range(4):
            emit(0, x, t, n_[x, t])
        return carry

    lax.fori_loop(0, 16, first, 0)
    pl.semaphore_wait(barrier, peers - 1)
    send(0, FAR)
    send(0, NEAR)

    loads[1].wait()
    loads[2].wait()

    def put_c(values, at):
        c_[at] = values

    def put_r(values, at):
        r_[at] = c_[at] * values

    place(cin, put_c)
    place(tin, put_r)
    acc[...] = jnp.zeros((8, 128), jnp.float32)

    def update0(x, t, smoothed, carry):
        n = n_[x, t]
        diag = n * smoothed * (1.0 / 32.0) + c_[x, t]
        inverse = jnp.where(diag > 0.0, 1.0 / jnp.where(diag > 0.0, diag, 1.0), 0.0)
        r = r_[x, t]
        p = inverse * r
        d_[x, t] = diag
        m_[x, t] = inverse
        p0_[x, t] = p
        emit(1, x, t, n * p)
        return (carry[0] + r * p,)

    def image(p_ref, x, t, smoothed):
        p, n = p_ref[x, t], n_[x, t]
        return p, n, d_[x, t] * p - n * smoothed * (1.0 / 32.0)

    def update1(x, t, smoothed, carry):
        p, n, u = image(p0_, x, t, smoothed)
        later = m_[x, t] * u - SHIFT * p
        u0_[x, t] = u
        p1_[x, t] = later
        emit(2, x, t, n * later)
        return carry[0] + u * p, carry[1] + u * later

    def update2(x, t, smoothed, carry):
        p, n, u = image(p1_, x, t, smoothed)
        later = m_[x, t] * u - SHIFT * p
        p2_[x, t] = later
        emit(3, x, t, n * later)
        return carry[0] + u * p, carry[1] + u0_[x, t] * later, carry[2] + u * later

    def update3(x, t, smoothed, carry):
        p, n, u = image(p2_, x, t, smoothed)
        return (carry[0] + u * p,)

    rows = 0
    for stage, (update, count) in enumerate(((update0, 1), (update1, 2), (update2, 3), (update3, 1))):
        receive(stage, NEAR)
        carry = spread(stage, (1, 2), update, (zero,) * count)
        receive(stage, FAR)
        carry = spread(stage, (0, 3), update, carry)
        if stage + 1 < STAGES:
            send(stage + 1, FAR)
            send(stage + 1, NEAR)
        for total in carry:
            keep_sum(rows, total)
            rows += 1

    each_peer(
        lambda r: pltpu.make_async_remote_copy(
            src_ref=acc, dst_ref=gathered.at[r - 1], send_sem=sum_send, recv_sem=sum_recv,
            device_id=peer_id(r), device_id_type=MESH,
        ).start()
    )
    pltpu.make_async_copy(gathered, gathered, sum_recv).wait()
    total = acc[...] + jnp.sum(gathered[...], axis=0)
    total = jnp.sum(total, axis=1, keepdims=True)
    b0, g00, g01, g11, g02, g12, g22 = (total[i : i + 1] for i in range(7))
    b1 = g00 - SHIFT * b0
    b2 = g01 - SHIFT * b1
    l10, l20 = g01 / g00, g02 / g00
    d1 = g11 - l10 * g01
    e12 = g12 - l20 * g01
    l21 = e12 / d1
    d2 = g22 - l20 * g02 - l21 * e12
    y1 = b1 - l10 * b0
    y2 = b2 - l20 * b0 - l21 * y1
    x2 = y2 / d2
    x1 = y1 / d1 - l21 * x2
    x0 = b0 / g00 - l10 * x1 - l20 * x2
    w0, w1, w2 = (jnp.broadcast_to(v, (8, 128)) for v in (x0, x1, x2))

    def combine(i, carry):
        for s in range(8):
            rt, rl, rx = s // 4, (s // 2) % 2, s % 2
            for lx in range(2):
                at = (rx * 2 + lx, rt * 8 + i, pl.ds(rl * 8, 8))
                bricks[s, i, pl.ds(lx, 8, stride=2), :] = w0 * p0_[at] + w1 * p1_[at] + w2 * p2_[at]
        for k in range(4):
            out[k, i] = bricks[slots[0, 0, 0, k], i] * kept[k]
        return carry

    kept = [jnp.where(k < counts[0, 0, 0], 1.0, 0.0) for k in range(4)]
    lax.fori_loop(0, 8, combine, 0)

    for stage in range(STAGES):
        for which in MESSAGES:
            guarded(which, 1, lambda which=which: message(stage, which).wait_send())
    pltpu.make_async_copy(gathered, gathered, sum_send).wait()


def per_device(nx, nt, target, confidence, normalizer, brick_slots, brick_counts):
    shape = (4, 8, 16, 128)
    whole = (4, 16, 16, 128)
    peers = nx * nt * 2
    vmem = lambda *dims: pltpu.VMEM(dims, jnp.float32)
    smem = pl.BlockSpec(memory_space=pltpu.SMEM)
    anywhere = pl.BlockSpec(memory_space=pl.ANY)
    out = pl.pallas_call(
        functools.partial(kernel, nx, nt),
        out_shape=jax.ShapeDtypeStruct(shape, jnp.float32),
        in_specs=[smem, smem, anywhere, anywhere, anywhere],
        out_specs=pl.BlockSpec(memory_space=pltpu.VMEM),
        scratch_shapes=[vmem(*shape)] * 3
        + [vmem(8, 8, 16, 128)]
        + [vmem(*whole)] * 9
        + [
            vmem(STAGES, 6, 18, 16, 128),
            vmem(STAGES, 4, 16, 128),
            vmem(STAGES, 6, 32, 128),
            vmem(4, 32, 128),
            vmem(4, 16, 128),
            vmem(8, 128),
            vmem(peers - 1, 8, 128),
            pltpu.SemaphoreType.DMA((3,)),
            pltpu.SemaphoreType.DMA((STAGES, len(MESSAGES))),
            pltpu.SemaphoreType.DMA((STAGES, len(MESSAGES))),
            pltpu.SemaphoreType.DMA,
            pltpu.SemaphoreType.DMA,
        ],
        compiler_params=pltpu.CompilerParams(
            collective_id=0, has_side_effects=True, vmem_limit_bytes=32 * 1024 * 1024
        ),
    )(
        brick_slots, brick_counts,
        target.reshape(shape), confidence.reshape(shape), normalizer.reshape(shape),
    )
    return out.reshape(target.shape)


def solution(mesh):
    split = P(("clip", "xt"), "tb", "luma", None, None, None, None, None)
    in_specs = (
        split,
        split,
        split,
        P(("clip", "xt"), "tb", "luma", None),
        P(("clip", "xt"), "tb", "luma"),
    )
    return jax.shard_map(
        functools.partial(per_device, mesh.shape["xt"], mesh.shape["tb"]),
        mesh=mesh, in_specs=in_specs, out_specs=split, check_vma=False,
    )
```

```python
import functools

import jax
import jax.numpy as jnp
from jax import lax
from jax.experimental import pallas as pl
from jax.experimental.pallas import tpu as pltpu
from jax.sharding import PartitionSpec as P

MESH = pl.DeviceIdType.MESH
SHIFT = 0.5
STAGES = 4
UNROLL = 4
SIDES = (-1, 0, 1)
MESSAGES = [(dx, dt, dl) for dl in (0, 1) for dx in SIDES for dt in SIDES if (dx, dt, dl) != (0, 0, 0)]
NEAR = [m for m in MESSAGES if m[0] == 0]
FAR = [m for m in MESSAGES if m[0] != 0]


def kernel(
    nx, nt,
    slots, counts, target, confidence, normalizer, out,
    tin, cin, nin, bricks, n_, c_, r_, d_, m_, p0_, p1_, p2_, u0_,
    q0, q1, q2, q3, es0, es1, es2, es3, er0, er1, er2, er3, fs, ff, acc, gathered,
    in_sem, send_sem, recv_sem, sum_send, sum_recv,
):
    ix, it, il = lax.axis_index("xt"), lax.axis_index("tb"), lax.axis_index("luma")
    q_, es, er = (q0, q1, q2, q3), (es0, es1, es2, es3), (er0, er1, er2, er3)
    peers = nx * nt * 2
    me = (ix * nt + it) * 2 + il

    loads = [
        pltpu.make_async_copy(src, dst, in_sem.at[i])
        for i, (src, dst) in enumerate(((normalizer, nin), (confidence, cin), (target, tin)))
    ]
    for load in loads:
        load.start()

    @pl.when(ix == 0)
    def _():
        for q, e in zip(q_, er):
            q[0] = jnp.zeros_like(q[0])
            e[0] = jnp.zeros_like(e[0])

    @pl.when(ix == nx - 1)
    def _():
        for q, e in zip(q_, er):
            q[5] = jnp.zeros_like(q[5])
            e[5] = jnp.zeros_like(e[5])

    @pl.when(it == 0)
    def _():
        for q, e in zip(q_, er):
            q[:, 0] = jnp.zeros_like(q[:, 0])
            e[:, 0:8] = jnp.zeros_like(e[:, 0:8])

    @pl.when(it == nt - 1)
    def _():
        for q, e in zip(q_, er):
            q[:, 17] = jnp.zeros_like(q[:, 17])
            e[:, 24:32] = jnp.zeros_like(e[:, 24:32])

    def peer_id(r):
        other = lax.rem(me + r, peers)
        return {"xt": lax.div(other, 2 * nt), "tb": lax.rem(lax.div(other, 2), nt), "luma": lax.rem(other, 2)}

    def each_peer(act):
        if peers <= 16:
            for r in range(1, peers):
                act(r)
        else:
            def step(r, carry):
                act(r)
                return carry
            lax.fori_loop(1, peers, step, 0)

    barrier = pltpu.get_barrier_semaphore()
    each_peer(lambda r: pl.semaphore_signal(barrier, inc=1, device_id=peer_id(r), device_id_type=MESH))

    row = lax.broadcasted_iota(jnp.int32, (16, 128), 0)
    col = lax.broadcasted_iota(jnp.int32, (16, 128), 1)
    edge = jnp.where(row == jnp.where(il == 0, 15, 0), 1.0, 0.0).astype(jnp.float32)
    zero = jnp.zeros((16, 128), jnp.float32)

    entry, here = [], []
    for s in range(8):
        k_s, h_s = jnp.int32(0), jnp.float32(0.0)
        for k in range(4):
            hit = jnp.logical_and(slots[0, 0, 0, k] == s, k < counts[0, 0, 0])
            k_s = jnp.where(hit, k, k_s)
            h_s = jnp.where(hit, 1.0, h_s)
        entry.append(k_s)
        here.append(h_s)

    def place(source, body):
        def step(i, carry):
            for s in range(8):
                bricks[s, i] = source[entry[s], i] * here[s]
            for s in range(8):
                rt, rl, rx = s // 4, (s // 2) % 2, s % 2
                for lx in range(2):
                    values = bricks[s, i, pl.ds(lx, 8, stride=2), :]
                    body(values, (rx * 2 + lx, rt * 8 + i, pl.ds(rl * 8, 8)))
            return carry
        lax.fori_loop(0, 8, step, 0)

    def emit(stage, x, t, values):
        tile = (
            2.0 * values
            + jnp.where(col == 0, 0.0, pltpu.roll(values, 1, 1))
            + jnp.where(col == 127, 0.0, pltpu.roll(values, 127, 1))
        )
        q_[stage][x + 1, t + 1] = tile
        es[stage][x, pl.ds(t, 1), :] = jnp.where(il == 0, tile[15:16], tile[0:1])

    def message(stage, which):
        dx, dt, dl = which
        i = MESSAGES.index(which)
        to = {"xt": ix + dx, "tb": it + dt, "luma": 1 - il if dl else il}
        if dl == 0:
            xs = {1: (4, 0), -1: (1, 5), 0: (pl.ds(1, 4), pl.ds(1, 4))}[dx]
            ts = {1: (16, 0), -1: (1, 17), 0: (pl.ds(1, 16), pl.ds(1, 16))}[dt]
            src, dst = (q_[stage].at[xs[j], ts[j]] for j in (0, 1))
        else:
            xs = {1: (3, 0), -1: (0, 5), 0: (pl.ds(0, 4), pl.ds(1, 4))}[dx]
            ts = {
                1: (pl.ds(8, 8), pl.ds(0, 8)),
                -1: (pl.ds(0, 8), pl.ds(24, 8)),
                0: (pl.ds(0, 16), pl.ds(8, 16)),
            }[dt]
            src, dst = es[stage].at[xs[0], ts[0]], er[stage].at[xs[1], ts[1]]
        return pltpu.make_async_remote_copy(
            src_ref=src, dst_ref=dst, send_sem=send_sem.at[stage, i], recv_sem=recv_sem.at[stage, i],
            device_id=to, device_id_type=MESH,
        )

    def guarded(which, sign, act):
        dx, dt, _ = which
        conds = []
        for d, at, size in ((dx * sign, ix, nx), (dt * sign, it, nt)):
            if d == 1:
                conds.append(at < size - 1)
            elif d == -1:
                conds.append(at > 0)
        if conds:
            pl.when(functools.reduce(jnp.logical_and, conds))(act)
        else:
            act()

    def send(stage, group):
        for which in group:
            guarded(which, 1, lambda which=which: message(stage, which).start())

    def receive(stage, group):
        for which in group:
            guarded(which, -1, lambda which=which: message(stage, which).wait_recv())

    def spread(stage, xs, update, carry):
        for x in xs:
            g = er[stage][x] + 2.0 * er[stage][x + 1] + er[stage][x + 2]
            fs[x] = g
            ff[x] = fs[x, pl.ds(7, 16)] + 2.0 * fs[x, pl.ds(8, 16)] + fs[x, pl.ds(9, 16)]
        need = sorted({x + d for x in xs for d in (0, 1, 2)})

        q = q_[stage]

        def step(i, carry):
            for t in (UNROLL * i + j for j in range(UNROLL)):
                sums = {x: q[x, t] + 2.0 * q[x, t + 1] + q[x, t + 2] for x in need}
                for x in xs:
                    a = sums[x] + 2.0 * sums[x + 1] + sums[x + 2]
                    smoothed = (
                        2.0 * a
                        + jnp.where(row == 0, 0.0, pltpu.roll(a, 1, 0))
                        + jnp.where(row == 15, 0.0, pltpu.roll(a, 15, 0))
                        + edge * ff[x, pl.ds(t, 1), :]
                    )
                    carry = update(x, t, smoothed, carry)
            return carry

        return lax.fori_loop(0, 16 // UNROLL, step, carry)

    def keep_sum(i, total):
        acc[pl.ds(i, 1), :] = jnp.sum(total, axis=0, keepdims=True)

    loads[0].wait()

    def put_n(values, at):
        n_[at] = values

    place(nin, put_n)

    def first(i, carry):
        for t in (UNROLL * i + j for j in range(UNROLL)):
            for x in range(4):
                emit(0, x, t, n_[x, t])
        return carry

    lax.fori_loop(0, 16 // UNROLL, first, 0)
    pl.semaphore_wait(barrier, peers - 1)
    send(0, FAR)
    send(0, NEAR)

    loads[1].wait()
    loads[2].wait()

    def put_c(values, at):
        c_[at] = values

    def put_r(values, at):
        r_[at] = c_[at] * values

    place(cin, put_c)
    place(tin, put_r)
    acc[...] = jnp.zeros((8, 128), jnp.float32)

    def update0(x, t, smoothed, carry):
        n = n_[x, t]
        diag = n * smoothed * (1.0 / 32.0) + c_[x, t]
        inverse = jnp.where(diag > 0.0, 1.0 / jnp.where(diag > 0.0, diag, 1.0), 0.0)
        r = r_[x, t]
        p = inverse * r
        d_[x, t] = diag
        m_[x, t] = inverse
        p0_[x, t] = p
        emit(1, x, t, n * p)
        return (carry[0] + r * p,)

    def image(p_ref, x, t, smoothed):
        p, n = p_ref[x, t], n_[x, t]
        return p, n, d_[x, t] * p - n * smoothed * (1.0 / 32.0)

    def update1(x, t, smoothed, carry):
        p, n, u = image(p0_, x, t, smoothed)
        later = m_[x, t] * u - SHIFT * p
        u0_[x, t] = u
        p1_[x, t] = later
        emit(2, x, t, n * later)
        return carry[0] + u * p, carry[1] + u * later

    def update2(x, t, smoothed, carry):
        p, n, u = image(p1_, x, t, smoothed)
        later = m_[x, t] * u - SHIFT * p
        p2_[x, t] = later
        emit(3, x, t, n * later)
        return carry[0] + u * p, carry[1] + u0_[x, t] * later, carry[2] + u * later

    def update3(x, t, smoothed, carry):
        p, n, u = image(p2_, x, t, smoothed)
        return (carry[0] + u * p,)

    rows = 0
    for stage, (update, count) in enumerate(((update0, 1), (update1, 2), (update2, 3), (update3, 1))):
        receive(stage, NEAR)
        carry = spread(stage, (1, 2), update, (zero,) * count)
        receive(stage, FAR)
        carry = spread(stage, (0, 3), update, carry)
        if stage + 1 < STAGES:
            send(stage + 1, FAR)
            send(stage + 1, NEAR)
        for total in carry:
            keep_sum(rows, total)
            rows += 1

    each_peer(
        lambda r: pltpu.make_async_remote_copy(
            src_ref=acc, dst_ref=gathered.at[r - 1], send_sem=sum_send, recv_sem=sum_recv,
            device_id=peer_id(r), device_id_type=MESH,
        ).start()
    )
    pltpu.make_async_copy(gathered, gathered, sum_recv).wait()
    total = acc[...] + jnp.sum(gathered[...], axis=0)
    total = jnp.sum(total, axis=1, keepdims=True)
    b0, g00, g01, g11, g02, g12, g22 = (total[i : i + 1] for i in range(7))
    b1 = g00 - SHIFT * b0
    b2 = g01 - SHIFT * b1
    l10, l20 = g01 / g00, g02 / g00
    d1 = g11 - l10 * g01
    e12 = g12 - l20 * g01
    l21 = e12 / d1
    d2 = g22 - l20 * g02 - l21 * e12
    y1 = b1 - l10 * b0
    y2 = b2 - l20 * b0 - l21 * y1
    x2 = y2 / d2
    x1 = y1 / d1 - l21 * x2
    x0 = b0 / g00 - l10 * x1 - l20 * x2
    w0, w1, w2 = (jnp.broadcast_to(v, (8, 128)) for v in (x0, x1, x2))

    def combine(i, carry):
        for s in range(8):
            rt, rl, rx = s // 4, (s // 2) % 2, s % 2
            for lx in range(2):
                at = (rx * 2 + lx, rt * 8 + i, pl.ds(rl * 8, 8))
                bricks[s, i, pl.ds(lx, 8, stride=2), :] = w0 * p0_[at] + w1 * p1_[at] + w2 * p2_[at]
        for k in range(4):
            out[k, i] = bricks[slots[0, 0, 0, k], i] * kept[k]
        return carry

    kept = [jnp.where(k < counts[0, 0, 0], 1.0, 0.0) for k in range(4)]
    lax.fori_loop(0, 8, combine, 0)

    for stage in range(STAGES):
        for which in MESSAGES:
            guarded(which, 1, lambda which=which: message(stage, which).wait_send())
    pltpu.make_async_copy(gathered, gathered, sum_send).wait()


def per_device(nx, nt, target, confidence, normalizer, brick_slots, brick_counts):
    shape = (4, 8, 16, 128)
    whole = (4, 16, 16, 128)
    peers = nx * nt * 2
    vmem = lambda *dims: pltpu.VMEM(dims, jnp.float32)
    smem = pl.BlockSpec(memory_space=pltpu.SMEM)
    anywhere = pl.BlockSpec(memory_space=pl.ANY)
    out = pl.pallas_call(
        functools.partial(kernel, nx, nt),
        out_shape=jax.ShapeDtypeStruct(shape, jnp.float32),
        in_specs=[smem, smem, anywhere, anywhere, anywhere],
        out_specs=pl.BlockSpec(memory_space=pltpu.VMEM),
        scratch_shapes=[vmem(*shape)] * 3
        + [vmem(8, 8, 16, 128)]
        + [vmem(*whole)] * 9
        + [vmem(6, 18, 16, 128)] * STAGES
        + [vmem(4, 16, 128)] * STAGES
        + [vmem(6, 32, 128)] * STAGES
        + [
            vmem(4, 32, 128),
            vmem(4, 16, 128),
            vmem(8, 128),
            vmem(peers - 1, 8, 128),
            pltpu.SemaphoreType.DMA((3,)),
            pltpu.SemaphoreType.DMA((STAGES, len(MESSAGES))),
            pltpu.SemaphoreType.DMA((STAGES, len(MESSAGES))),
            pltpu.SemaphoreType.DMA,
            pltpu.SemaphoreType.DMA,
        ],
        compiler_params=pltpu.CompilerParams(
            collective_id=0, has_side_effects=True, vmem_limit_bytes=60 * 1024 * 1024
        ),
    )(
        brick_slots, brick_counts,
        target.reshape(shape), confidence.reshape(shape), normalizer.reshape(shape),
    )
    return out.reshape(target.shape)


def solution(mesh):
    split = P(("clip", "xt"), "tb", "luma", None, None, None, None, None)
    in_specs = (
        split,
        split,
        split,
        P(("clip", "xt"), "tb", "luma", None),
        P(("clip", "xt"), "tb", "luma"),
    )
    return jax.shard_map(
        functools.partial(per_device, mesh.shape["xt"], mesh.shape["tb"]),
        mesh=mesh, in_specs=in_specs, out_specs=split, check_vma=False,
    )
```

```python
import functools

import jax
import jax.numpy as jnp
from jax import lax
from jax.experimental import pallas as pl
from jax.experimental.pallas import tpu as pltpu
from jax.sharding import PartitionSpec as P

MESH = pl.DeviceIdType.MESH
SHIFT = 0.5
STAGES = 4
UNROLL = 8
SIDES = (-1, 0, 1)
MESSAGES = [(dx, dt, dl) for dl in (0, 1) for dx in SIDES for dt in SIDES if (dx, dt, dl) != (0, 0, 0)]
NEAR = [m for m in MESSAGES if m[0] == 0]
FACES = [(1, 0, 0), (-1, 0, 0)]
FAR = FACES + [m for m in MESSAGES if m[0] != 0 and m not in FACES]
SEND_ORDER = FACES + NEAR + FAR[2:]


def kernel(
    nx, nt,
    slots, counts, target, confidence, normalizer, out,
    tin, cin, nin, bricks, n_, c_, r_, d_, m_, p0_, p1_, p2_, u0_,
    q0, q1, q2, q3, es0, es1, es2, es3, er0, er1, er2, er3, fs, ff, acc, gathered,
    in_sem, send_sem, recv_sem, sum_send, sum_recv,
):
    ix, it, il = lax.axis_index("xt"), lax.axis_index("tb"), lax.axis_index("luma")
    q_, es, er = (q0, q1, q2, q3), (es0, es1, es2, es3), (er0, er1, er2, er3)
    peers = nx * nt * 2
    me = (ix * nt + it) * 2 + il

    loads = [
        pltpu.make_async_copy(src, dst, in_sem.at[i])
        for i, (src, dst) in enumerate(((normalizer, nin), (confidence, cin), (target, tin)))
    ]
    for load in loads:
        load.start()

    @pl.when(ix == 0)
    def _():
        for q, e in zip(q_, er):
            q[0] = jnp.zeros_like(q[0])
            e[0] = jnp.zeros_like(e[0])

    @pl.when(ix == nx - 1)
    def _():
        for q, e in zip(q_, er):
            q[5] = jnp.zeros_like(q[5])
            e[5] = jnp.zeros_like(e[5])

    @pl.when(it == 0)
    def _():
        for q, e in zip(q_, er):
            q[:, 0] = jnp.zeros_like(q[:, 0])
            e[:, 0:8] = jnp.zeros_like(e[:, 0:8])

    @pl.when(it == nt - 1)
    def _():
        for q, e in zip(q_, er):
            q[:, 17] = jnp.zeros_like(q[:, 17])
            e[:, 24:32] = jnp.zeros_like(e[:, 24:32])

    def peer_id(r):
        other = lax.rem(me + r, peers)
        return {"xt": lax.div(other, 2 * nt), "tb": lax.rem(lax.div(other, 2), nt), "luma": lax.rem(other, 2)}

    def each_peer(act):
        if peers <= 16:
            for r in range(1, peers):
                act(r)
        else:
            def step(r, carry):
                act(r)
                return carry
            lax.fori_loop(1, peers, step, 0)

    barrier = pltpu.get_barrier_semaphore()
    each_peer(lambda r: pl.semaphore_signal(barrier, inc=1, device_id=peer_id(r), device_id_type=MESH))

    row = lax.broadcasted_iota(jnp.int32, (16, 128), 0)
    col = lax.broadcasted_iota(jnp.int32, (16, 128), 1)
    edge = jnp.where(row == jnp.where(il == 0, 15, 0), 1.0, 0.0).astype(jnp.float32)
    zero = jnp.zeros((16, 128), jnp.float32)

    entry, here = [], []
    for s in range(8):
        k_s, h_s = jnp.int32(0), jnp.float32(0.0)
        for k in range(4):
            hit = jnp.logical_and(slots[0, 0, 0, k] == s, k < counts[0, 0, 0])
            k_s = jnp.where(hit, k, k_s)
            h_s = jnp.where(hit, 1.0, h_s)
        entry.append(k_s)
        here.append(h_s)

    def place(source, body):
        def step(i, carry):
            for s in range(8):
                bricks[s, i] = source[entry[s], i] * here[s]
            for s in range(8):
                rt, rl, rx = s // 4, (s // 2) % 2, s % 2
                for lx in range(2):
                    values = bricks[s, i, pl.ds(lx, 8, stride=2), :]
                    body(values, (rx * 2 + lx, rt * 8 + i, pl.ds(rl * 8, 8)))
            return carry
        lax.fori_loop(0, 8, step, 0)

    def emit(stage, x, t, values):
        tile = (
            2.0 * values
            + jnp.where(col == 0, 0.0, pltpu.roll(values, 1, 1))
            + jnp.where(col == 127, 0.0, pltpu.roll(values, 127, 1))
        )
        q_[stage][x + 1, t + 1] = tile
        es[stage][x, pl.ds(t, 1), :] = jnp.where(il == 0, tile[15:16], tile[0:1])

    def message(stage, which):
        dx, dt, dl = which
        i = MESSAGES.index(which)
        to = {"xt": ix + dx, "tb": it + dt, "luma": 1 - il if dl else il}
        if dl == 0:
            xs = {1: (4, 0), -1: (1, 5), 0: (pl.ds(1, 4), pl.ds(1, 4))}[dx]
            ts = {1: (16, 0), -1: (1, 17), 0: (pl.ds(1, 16), pl.ds(1, 16))}[dt]
            src, dst = (q_[stage].at[xs[j], ts[j]] for j in (0, 1))
        else:
            xs = {1: (3, 0), -1: (0, 5), 0: (pl.ds(0, 4), pl.ds(1, 4))}[dx]
            ts = {
                1: (pl.ds(8, 8), pl.ds(0, 8)),
                -1: (pl.ds(0, 8), pl.ds(24, 8)),
                0: (pl.ds(0, 16), pl.ds(8, 16)),
            }[dt]
            src, dst = es[stage].at[xs[0], ts[0]], er[stage].at[xs[1], ts[1]]
        return pltpu.make_async_remote_copy(
            src_ref=src, dst_ref=dst, send_sem=send_sem.at[stage, i], recv_sem=recv_sem.at[stage, i],
            device_id=to, device_id_type=MESH,
        )

    def guarded(which, sign, act):
        dx, dt, _ = which
        conds = []
        for d, at, size in ((dx * sign, ix, nx), (dt * sign, it, nt)):
            if d == 1:
                conds.append(at < size - 1)
            elif d == -1:
                conds.append(at > 0)
        if conds:
            pl.when(functools.reduce(jnp.logical_and, conds))(act)
        else:
            act()

    def send(stage, group):
        for which in group:
            guarded(which, 1, lambda which=which: message(stage, which).start())

    def receive(stage, group):
        for which in group:
            guarded(which, -1, lambda which=which: message(stage, which).wait_recv())

    def spread(stage, xs, update, carry):
        for x in xs:
            g = er[stage][x] + 2.0 * er[stage][x + 1] + er[stage][x + 2]
            fs[x] = g
            ff[x] = fs[x, pl.ds(7, 16)] + 2.0 * fs[x, pl.ds(8, 16)] + fs[x, pl.ds(9, 16)]
        need = sorted({x + d for x in xs for d in (0, 1, 2)})

        q = q_[stage]

        def step(i, carry):
            for t in (UNROLL * i + j for j in range(UNROLL)):
                sums = {x: q[x, t] + 2.0 * q[x, t + 1] + q[x, t + 2] for x in need}
                for x in xs:
                    a = sums[x] + 2.0 * sums[x + 1] + sums[x + 2]
                    smoothed = (
                        2.0 * a
                        + jnp.where(row == 0, 0.0, pltpu.roll(a, 1, 0))
                        + jnp.where(row == 15, 0.0, pltpu.roll(a, 15, 0))
                        + edge * ff[x, pl.ds(t, 1), :]
                    )
                    carry = update(x, t, smoothed, carry)
            return carry

        return lax.fori_loop(0, 16 // UNROLL, step, carry)

    def keep_sum(i, total):
        acc[pl.ds(i, 1), :] = jnp.sum(total, axis=0, keepdims=True)

    loads[0].wait()

    def put_n(values, at):
        n_[at] = values

    place(nin, put_n)

    def first(i, carry):
        for t in (UNROLL * i + j for j in range(UNROLL)):
            for x in range(4):
                emit(0, x, t, n_[x, t])
        return carry

    lax.fori_loop(0, 16 // UNROLL, first, 0)
    pl.semaphore_wait(barrier, peers - 1)
    send(0, SEND_ORDER)

    loads[1].wait()
    loads[2].wait()

    def put_c(values, at):
        c_[at] = values

    def put_r(values, at):
        r_[at] = c_[at] * values

    place(cin, put_c)
    place(tin, put_r)
    acc[...] = jnp.zeros((8, 128), jnp.float32)

    def update0(x, t, smoothed, carry):
        n = n_[x, t]
        diag = n * smoothed * (1.0 / 32.0) + c_[x, t]
        inverse = jnp.where(diag > 0.0, 1.0 / jnp.where(diag > 0.0, diag, 1.0), 0.0)
        r = r_[x, t]
        p = inverse * r
        d_[x, t] = diag
        m_[x, t] = inverse
        p0_[x, t] = p
        emit(1, x, t, n * p)
        return (carry[0] + r * p,)

    def image(p_ref, x, t, smoothed):
        p, n = p_ref[x, t], n_[x, t]
        return p, n, d_[x, t] * p - n * smoothed * (1.0 / 32.0)

    def update1(x, t, smoothed, carry):
        p, n, u = image(p0_, x, t, smoothed)
        later = m_[x, t] * u - SHIFT * p
        u0_[x, t] = u
        p1_[x, t] = later
        emit(2, x, t, n * later)
        return carry[0] + u * p, carry[1] + u * later

    def update2(x, t, smoothed, carry):
        p, n, u = image(p1_, x, t, smoothed)
        later = m_[x, t] * u - SHIFT * p
        p2_[x, t] = later
        emit(3, x, t, n * later)
        return carry[0] + u * p, carry[1] + u0_[x, t] * later, carry[2] + u * later

    def update3(x, t, smoothed, carry):
        p, n, u = image(p2_, x, t, smoothed)
        return (carry[0] + u * p,)

    rows = 0
    for stage, (update, count) in enumerate(((update0, 1), (update1, 2), (update2, 3), (update3, 1))):
        receive(stage, NEAR)
        carry = spread(stage, (1, 2), update, (zero,) * count)
        receive(stage, FAR)
        carry = spread(stage, (0, 3), update, carry)
        if stage + 1 < STAGES:
            send(stage + 1, SEND_ORDER)
        for total in carry:
            keep_sum(rows, total)
            rows += 1

    each_peer(
        lambda r: pltpu.make_async_remote_copy(
            src_ref=acc, dst_ref=gathered.at[r - 1], send_sem=sum_send, recv_sem=sum_recv,
            device_id=peer_id(r), device_id_type=MESH,
        ).start()
    )
    pltpu.make_async_copy(gathered, gathered, sum_recv).wait()
    total = acc[...] + jnp.sum(gathered[...], axis=0)
    total = jnp.sum(total, axis=1, keepdims=True)
    b0, g00, g01, g11, g02, g12, g22 = (total[i : i + 1] for i in range(7))
    b1 = g00 - SHIFT * b0
    b2 = g01 - SHIFT * b1
    l10, l20 = g01 / g00, g02 / g00
    d1 = g11 - l10 * g01
    e12 = g12 - l20 * g01
    l21 = e12 / d1
    d2 = g22 - l20 * g02 - l21 * e12
    y1 = b1 - l10 * b0
    y2 = b2 - l20 * b0 - l21 * y1
    x2 = y2 / d2
    x1 = y1 / d1 - l21 * x2
    x0 = b0 / g00 - l10 * x1 - l20 * x2
    w0, w1, w2 = (jnp.broadcast_to(v, (8, 128)) for v in (x0, x1, x2))

    def combine(i, carry):
        for s in range(8):
            rt, rl, rx = s // 4, (s // 2) % 2, s % 2
            for lx in range(2):
                at = (rx * 2 + lx, rt * 8 + i, pl.ds(rl * 8, 8))
                bricks[s, i, pl.ds(lx, 8, stride=2), :] = w0 * p0_[at] + w1 * p1_[at] + w2 * p2_[at]
        for k in range(4):
            out[k, i] = bricks[slots[0, 0, 0, k], i] * kept[k]
        return carry

    kept = [jnp.where(k < counts[0, 0, 0], 1.0, 0.0) for k in range(4)]
    lax.fori_loop(0, 8, combine, 0)

    for stage in range(STAGES):
        for which in MESSAGES:
            guarded(which, 1, lambda which=which: message(stage, which).wait_send())
    pltpu.make_async_copy(gathered, gathered, sum_send).wait()


def per_device(nx, nt, target, confidence, normalizer, brick_slots, brick_counts):
    shape = (4, 8, 16, 128)
    whole = (4, 16, 16, 128)
    peers = nx * nt * 2
    vmem = lambda *dims: pltpu.VMEM(dims, jnp.float32)
    smem = pl.BlockSpec(memory_space=pltpu.SMEM)
    anywhere = pl.BlockSpec(memory_space=pl.ANY)
    out = pl.pallas_call(
        functools.partial(kernel, nx, nt),
        out_shape=jax.ShapeDtypeStruct(shape, jnp.float32),
        in_specs=[smem, smem, anywhere, anywhere, anywhere],
        out_specs=pl.BlockSpec(memory_space=pltpu.VMEM),
        scratch_shapes=[vmem(*shape)] * 3
        + [vmem(8, 8, 16, 128)]
        + [vmem(*whole)] * 9
        + [vmem(6, 18, 16, 128)] * STAGES
        + [vmem(4, 16, 128)] * STAGES
        + [vmem(6, 32, 128)] * STAGES
        + [
            vmem(4, 32, 128),
            vmem(4, 16, 128),
            vmem(8, 128),
            vmem(peers - 1, 8, 128),
            pltpu.SemaphoreType.DMA((3,)),
            pltpu.SemaphoreType.DMA((STAGES, len(MESSAGES))),
            pltpu.SemaphoreType.DMA((STAGES, len(MESSAGES))),
            pltpu.SemaphoreType.DMA,
            pltpu.SemaphoreType.DMA,
        ],
        compiler_params=pltpu.CompilerParams(
            collective_id=0, has_side_effects=True, vmem_limit_bytes=60 * 1024 * 1024
        ),
    )(
        brick_slots, brick_counts,
        target.reshape(shape), confidence.reshape(shape), normalizer.reshape(shape),
    )
    return out.reshape(target.shape)


def solution(mesh):
    split = P(("clip", "xt"), "tb", "luma", None, None, None, None, None)
    in_specs = (
        split,
        split,
        split,
        P(("clip", "xt"), "tb", "luma", None),
        P(("clip", "xt"), "tb", "luma"),
    )
    return jax.shard_map(
        functools.partial(per_device, mesh.shape["xt"], mesh.shape["tb"]),
        mesh=mesh, in_specs=in_specs, out_specs=split, check_vma=False,
    )
```

```python
import functools

import jax
import jax.numpy as jnp
from jax import lax
from jax.experimental import pallas as pl
from jax.experimental.pallas import tpu as pltpu
from jax.sharding import PartitionSpec as P

MESH = pl.DeviceIdType.MESH
SHIFT = 0.5
STAGES = 4
UNROLL = 8
SIDES = (-1, 0, 1)
MESSAGES = [(dx, dt, dl) for dl in (0, 1) for dx in SIDES for dt in SIDES if (dx, dt, dl) != (0, 0, 0)]
NEAR = [m for m in MESSAGES if m[0] == 0]
FAR = [m for m in MESSAGES if m[0] != 0]
SEND_ORDER = sorted(MESSAGES, key=lambda m: -abs(m[0]) - abs(m[1]) - m[2])


def kernel(
    nx, nt,
    slots, counts, target, confidence, normalizer, out,
    tin, cin, nin, bricks, n_, c_, r_, d_, m_, p0_, p1_, p2_, u0_,
    q0, q1, q2, q3, es0, es1, es2, es3, er0, er1, er2, er3, fs, ff, acc, gathered,
    in_sem, send_sem, recv_sem, sum_send, sum_recv,
):
    ix, it, il = lax.axis_index("xt"), lax.axis_index("tb"), lax.axis_index("luma")
    q_, es, er = (q0, q1, q2, q3), (es0, es1, es2, es3), (er0, er1, er2, er3)
    peers = nx * nt * 2
    me = (ix * nt + it) * 2 + il

    loads = [
        pltpu.make_async_copy(src, dst, in_sem.at[i])
        for i, (src, dst) in enumerate(((normalizer, nin), (confidence, cin), (target, tin)))
    ]
    for load in loads:
        load.start()

    @pl.when(ix == 0)
    def _():
        for q, e in zip(q_, er):
            q[0] = jnp.zeros_like(q[0])
            e[0] = jnp.zeros_like(e[0])

    @pl.when(ix == nx - 1)
    def _():
        for q, e in zip(q_, er):
            q[5] = jnp.zeros_like(q[5])
            e[5] = jnp.zeros_like(e[5])

    @pl.when(it == 0)
    def _():
        for q, e in zip(q_, er):
            q[:, 0] = jnp.zeros_like(q[:, 0])
            e[:, 0:8] = jnp.zeros_like(e[:, 0:8])

    @pl.when(it == nt - 1)
    def _():
        for q, e in zip(q_, er):
            q[:, 17] = jnp.zeros_like(q[:, 17])
            e[:, 24:32] = jnp.zeros_like(e[:, 24:32])

    def peer_id(r):
        other = lax.rem(me + r, peers)
        return {"xt": lax.div(other, 2 * nt), "tb": lax.rem(lax.div(other, 2), nt), "luma": lax.rem(other, 2)}

    def each_peer(act):
        if peers <= 16:
            for r in range(1, peers):
                act(r)
        else:
            def step(r, carry):
                act(r)
                return carry
            lax.fori_loop(1, peers, step, 0)

    barrier = pltpu.get_barrier_semaphore()
    each_peer(lambda r: pl.semaphore_signal(barrier, inc=1, device_id=peer_id(r), device_id_type=MESH))

    row = lax.broadcasted_iota(jnp.int32, (16, 128), 0)
    col = lax.broadcasted_iota(jnp.int32, (16, 128), 1)
    edge = jnp.where(row == jnp.where(il == 0, 15, 0), 1.0, 0.0).astype(jnp.float32)
    zero = jnp.zeros((16, 128), jnp.float32)

    entry, here = [], []
    for s in range(8):
        k_s, h_s = jnp.int32(0), jnp.float32(0.0)
        for k in range(4):
            hit = jnp.logical_and(slots[0, 0, 0, k] == s, k < counts[0, 0, 0])
            k_s = jnp.where(hit, k, k_s)
            h_s = jnp.where(hit, 1.0, h_s)
        entry.append(k_s)
        here.append(h_s)

    def place(source, body):
        def step(i, carry):
            for s in range(8):
                bricks[s, i] = source[entry[s], i] * here[s]
            for s in range(8):
                rt, rl, rx = s // 4, (s // 2) % 2, s % 2
                for lx in range(2):
                    values = bricks[s, i, pl.ds(lx, 8, stride=2), :]
                    body(values, (rx * 2 + lx, rt * 8 + i, pl.ds(rl * 8, 8)))
            return carry
        lax.fori_loop(0, 8, step, 0)

    def emit(stage, x, t, values):
        tile = (
            2.0 * values
            + jnp.where(col == 0, 0.0, pltpu.roll(values, 1, 1))
            + jnp.where(col == 127, 0.0, pltpu.roll(values, 127, 1))
        )
        q_[stage][x + 1, t + 1] = tile
        es[stage][x, pl.ds(t, 1), :] = jnp.where(il == 0, tile[15:16], tile[0:1])

    def message(stage, which):
        dx, dt, dl = which
        i = MESSAGES.index(which)
        to = {"xt": ix + dx, "tb": it + dt, "luma": 1 - il if dl else il}
        if dl == 0:
            xs = {1: (4, 0), -1: (1, 5), 0: (pl.ds(1, 4), pl.ds(1, 4))}[dx]
            ts = {1: (16, 0), -1: (1, 17), 0: (pl.ds(1, 16), pl.ds(1, 16))}[dt]
            src, dst = (q_[stage].at[xs[j], ts[j]] for j in (0, 1))
        else:
            xs = {1: (3, 0), -1: (0, 5), 0: (pl.ds(0, 4), pl.ds(1, 4))}[dx]
            ts = {
                1: (pl.ds(8, 8), pl.ds(0, 8)),
                -1: (pl.ds(0, 8), pl.ds(24, 8)),
                0: (pl.ds(0, 16), pl.ds(8, 16)),
            }[dt]
            src, dst = es[stage].at[xs[0], ts[0]], er[stage].at[xs[1], ts[1]]
        return pltpu.make_async_remote_copy(
            src_ref=src, dst_ref=dst, send_sem=send_sem.at[stage, i], recv_sem=recv_sem.at[stage, i],
            device_id=to, device_id_type=MESH,
        )

    def guarded(which, sign, act):
        dx, dt, _ = which
        conds = []
        for d, at, size in ((dx * sign, ix, nx), (dt * sign, it, nt)):
            if d == 1:
                conds.append(at < size - 1)
            elif d == -1:
                conds.append(at > 0)
        if conds:
            pl.when(functools.reduce(jnp.logical_and, conds))(act)
        else:
            act()

    def send(stage, group):
        for which in group:
            guarded(which, 1, lambda which=which: message(stage, which).start())

    def receive(stage, group):
        for which in group:
            guarded(which, -1, lambda which=which: message(stage, which).wait_recv())

    def spread(stage, xs, update, carry):
        for x in xs:
            g = er[stage][x] + 2.0 * er[stage][x + 1] + er[stage][x + 2]
            fs[x] = g
            ff[x] = fs[x, pl.ds(7, 16)] + 2.0 * fs[x, pl.ds(8, 16)] + fs[x, pl.ds(9, 16)]
        need = sorted({x + d for x in xs for d in (0, 1, 2)})

        q = q_[stage]

        def step(i, carry):
            for t in (UNROLL * i + j for j in range(UNROLL)):
                sums = {x: q[x, t] + 2.0 * q[x, t + 1] + q[x, t + 2] for x in need}
                for x in xs:
                    a = sums[x] + 2.0 * sums[x + 1] + sums[x + 2]
                    smoothed = (
                        2.0 * a
                        + jnp.where(row == 0, 0.0, pltpu.roll(a, 1, 0))
                        + jnp.where(row == 15, 0.0, pltpu.roll(a, 15, 0))
                        + edge * ff[x, pl.ds(t, 1), :]
                    )
                    carry = update(x, t, smoothed, carry)
            return carry

        return lax.fori_loop(0, 16 // UNROLL, step, carry)

    def keep_sum(i, total):
        acc[pl.ds(i, 1), :] = jnp.sum(total, axis=0, keepdims=True)

    loads[0].wait()

    def put_n(values, at):
        n_[at] = values

    place(nin, put_n)

    def first(i, carry):
        for t in (UNROLL * i + j for j in range(UNROLL)):
            for x in range(4):
                emit(0, x, t, n_[x, t])
        return carry

    lax.fori_loop(0, 16 // UNROLL, first, 0)
    pl.semaphore_wait(barrier, peers - 1)
    send(0, SEND_ORDER)

    loads[1].wait()
    loads[2].wait()

    def put_c(values, at):
        c_[at] = values

    def put_r(values, at):
        r_[at] = c_[at] * values

    place(cin, put_c)
    place(tin, put_r)
    acc[...] = jnp.zeros((8, 128), jnp.float32)

    def update0(x, t, smoothed, carry):
        n = n_[x, t]
        diag = n * smoothed * (1.0 / 32.0) + c_[x, t]
        inverse = jnp.where(diag > 0.0, 1.0 / jnp.where(diag > 0.0, diag, 1.0), 0.0)
        r = r_[x, t]
        p = inverse * r
        d_[x, t] = diag
        m_[x, t] = inverse
        p0_[x, t] = p
        emit(1, x, t, n * p)
        return (carry[0] + r * p,)

    def image(p_ref, x, t, smoothed):
        p, n = p_ref[x, t], n_[x, t]
        return p, n, d_[x, t] * p - n * smoothed * (1.0 / 32.0)

    def update1(x, t, smoothed, carry):
        p, n, u = image(p0_, x, t, smoothed)
        later = m_[x, t] * u - SHIFT * p
        u0_[x, t] = u
        p1_[x, t] = later
        emit(2, x, t, n * later)
        return carry[0] + u * p, carry[1] + u * later

    def update2(x, t, smoothed, carry):
        p, n, u = image(p1_, x, t, smoothed)
        later = m_[x, t] * u - SHIFT * p
        p2_[x, t] = later
        emit(3, x, t, n * later)
        return carry[0] + u * p, carry[1] + u0_[x, t] * later, carry[2] + u * later

    def update3(x, t, smoothed, carry):
        p, n, u = image(p2_, x, t, smoothed)
        return (carry[0] + u * p,)

    rows = 0
    for stage, (update, count) in enumerate(((update0, 1), (update1, 2), (update2, 3), (update3, 1))):
        receive(stage, NEAR)
        carry = spread(stage, (1, 2), update, (zero,) * count)
        receive(stage, FAR)
        carry = spread(stage, (0, 3), update, carry)
        if stage + 1 < STAGES:
            send(stage + 1, SEND_ORDER)
        for total in carry:
            keep_sum(rows, total)
            rows += 1

    each_peer(
        lambda r: pltpu.make_async_remote_copy(
            src_ref=acc, dst_ref=gathered.at[r - 1], send_sem=sum_send, recv_sem=sum_recv,
            device_id=peer_id(r), device_id_type=MESH,
        ).start()
    )
    pltpu.make_async_copy(gathered, gathered, sum_recv).wait()
    total = acc[...] + jnp.sum(gathered[...], axis=0)
    total = jnp.sum(total, axis=1, keepdims=True)
    b0, g00, g01, g11, g02, g12, g22 = (total[i : i + 1] for i in range(7))
    b1 = g00 - SHIFT * b0
    b2 = g01 - SHIFT * b1
    l10, l20 = g01 / g00, g02 / g00
    d1 = g11 - l10 * g01
    e12 = g12 - l20 * g01
    l21 = e12 / d1
    d2 = g22 - l20 * g02 - l21 * e12
    y1 = b1 - l10 * b0
    y2 = b2 - l20 * b0 - l21 * y1
    x2 = y2 / d2
    x1 = y1 / d1 - l21 * x2
    x0 = b0 / g00 - l10 * x1 - l20 * x2
    w0, w1, w2 = (jnp.broadcast_to(v, (8, 128)) for v in (x0, x1, x2))

    def combine(i, carry):
        for s in range(8):
            rt, rl, rx = s // 4, (s // 2) % 2, s % 2
            for lx in range(2):
                at = (rx * 2 + lx, rt * 8 + i, pl.ds(rl * 8, 8))
                bricks[s, i, pl.ds(lx, 8, stride=2), :] = w0 * p0_[at] + w1 * p1_[at] + w2 * p2_[at]
        for k in range(4):
            out[k, i] = bricks[slots[0, 0, 0, k], i] * kept[k]
        return carry

    kept = [jnp.where(k < counts[0, 0, 0], 1.0, 0.0) for k in range(4)]
    lax.fori_loop(0, 8, combine, 0)

    for stage in range(STAGES):
        for which in MESSAGES:
            guarded(which, 1, lambda which=which: message(stage, which).wait_send())
    pltpu.make_async_copy(gathered, gathered, sum_send).wait()


def per_device(nx, nt, target, confidence, normalizer, brick_slots, brick_counts):
    shape = (4, 8, 16, 128)
    whole = (4, 16, 16, 128)
    peers = nx * nt * 2
    vmem = lambda *dims: pltpu.VMEM(dims, jnp.float32)
    smem = pl.BlockSpec(memory_space=pltpu.SMEM)
    anywhere = pl.BlockSpec(memory_space=pl.ANY)
    out = pl.pallas_call(
        functools.partial(kernel, nx, nt),
        out_shape=jax.ShapeDtypeStruct(shape, jnp.float32),
        in_specs=[smem, smem, anywhere, anywhere, anywhere],
        out_specs=pl.BlockSpec(memory_space=pltpu.VMEM),
        scratch_shapes=[vmem(*shape)] * 3
        + [vmem(8, 8, 16, 128)]
        + [vmem(*whole)] * 9
        + [vmem(6, 18, 16, 128)] * STAGES
        + [vmem(4, 16, 128)] * STAGES
        + [vmem(6, 32, 128)] * STAGES
        + [
            vmem(4, 32, 128),
            vmem(4, 16, 128),
            vmem(8, 128),
            vmem(peers - 1, 8, 128),
            pltpu.SemaphoreType.DMA((3,)),
            pltpu.SemaphoreType.DMA((STAGES, len(MESSAGES))),
            pltpu.SemaphoreType.DMA((STAGES, len(MESSAGES))),
            pltpu.SemaphoreType.DMA,
            pltpu.SemaphoreType.DMA,
        ],
        compiler_params=pltpu.CompilerParams(
            collective_id=0, has_side_effects=True, vmem_limit_bytes=60 * 1024 * 1024
        ),
    )(
        brick_slots, brick_counts,
        target.reshape(shape), confidence.reshape(shape), normalizer.reshape(shape),
    )
    return out.reshape(target.shape)


def solution(mesh):
    split = P(("clip", "xt"), "tb", "luma", None, None, None, None, None)
    in_specs = (
        split,
        split,
        split,
        P(("clip", "xt"), "tb", "luma", None),
        P(("clip", "xt"), "tb", "luma"),
    )
    return jax.shard_map(
        functools.partial(per_device, mesh.shape["xt"], mesh.shape["tb"]),
        mesh=mesh, in_specs=in_specs, out_specs=split, check_vma=False,
    )
```

```python
import functools

import jax
import jax.numpy as jnp
from jax import lax
from jax.experimental import pallas as pl
from jax.experimental.pallas import tpu as pltpu
from jax.sharding import PartitionSpec as P

MESH = pl.DeviceIdType.MESH
SHIFT = 0.5
STAGES = 4
UNROLL = 8
SIDES = (-1, 0, 1)
MESSAGES = [(dx, dt, dl) for dl in (0, 1) for dx in SIDES for dt in SIDES if (dx, dt, dl) != (0, 0, 0)]
NEAR = [m for m in MESSAGES if m[0] == 0]
FAR = [m for m in MESSAGES if m[0] != 0]
SEND_ORDER = sorted(MESSAGES, key=lambda m: -abs(m[0]) - abs(m[1]) - m[2])


def kernel(
    nx, nt,
    slots, counts, target, confidence, normalizer, out,
    tin, cin, nin, bricks, n_, c_, r_, d_, m_, p0_, p1_, p2_, u0_,
    q0, q1, q2, q3, es0, es1, es2, es3, er0, er1, er2, er3, fs, ff, acc, gathered,
    in_sem, send_sem, recv_sem, sum_send, sum_recv,
):
    ix, it, il = lax.axis_index("xt"), lax.axis_index("tb"), lax.axis_index("luma")
    q_, es, er = (q0, q1, q2, q3), (es0, es1, es2, es3), (er0, er1, er2, er3)
    peers = nx * nt * 2
    me = (ix * nt + it) * 2 + il

    loads = [
        pltpu.make_async_copy(src, dst, in_sem.at[i])
        for i, (src, dst) in enumerate(((normalizer, nin), (confidence, cin), (target, tin)))
    ]
    for load in loads:
        load.start()

    @pl.when(ix == 0)
    def _():
        for q, e in zip(q_, er):
            q[0] = jnp.zeros_like(q[0])
            e[0] = jnp.zeros_like(e[0])

    @pl.when(ix == nx - 1)
    def _():
        for q, e in zip(q_, er):
            q[5] = jnp.zeros_like(q[5])
            e[5] = jnp.zeros_like(e[5])

    @pl.when(it == 0)
    def _():
        for q, e in zip(q_, er):
            q[:, 0] = jnp.zeros_like(q[:, 0])
            e[:, 0:8] = jnp.zeros_like(e[:, 0:8])

    @pl.when(it == nt - 1)
    def _():
        for q, e in zip(q_, er):
            q[:, 17] = jnp.zeros_like(q[:, 17])
            e[:, 24:32] = jnp.zeros_like(e[:, 24:32])

    def peer_id(r):
        other = lax.rem(me + r, peers)
        return {"xt": lax.div(other, 2 * nt), "tb": lax.rem(lax.div(other, 2), nt), "luma": lax.rem(other, 2)}

    def each_peer(act):
        if peers <= 16:
            for r in range(1, peers):
                act(r)
        else:
            def step(r, carry):
                act(r)
                return carry
            lax.fori_loop(1, peers, step, 0)

    barrier = pltpu.get_barrier_semaphore()
    each_peer(lambda r: pl.semaphore_signal(barrier, inc=1, device_id=peer_id(r), device_id_type=MESH))

    row = lax.broadcasted_iota(jnp.int32, (16, 128), 0)
    col = lax.broadcasted_iota(jnp.int32, (16, 128), 1)
    edge = jnp.where(row == jnp.where(il == 0, 15, 0), 1.0, 0.0).astype(jnp.float32)
    zero = jnp.zeros((16, 128), jnp.float32)

    entry, here = [], []
    for s in range(8):
        k_s, h_s = jnp.int32(0), jnp.float32(0.0)
        for k in range(4):
            hit = jnp.logical_and(slots[0, 0, 0, k] == s, k < counts[0, 0, 0])
            k_s = jnp.where(hit, k, k_s)
            h_s = jnp.where(hit, 1.0, h_s)
        entry.append(k_s)
        here.append(h_s)

    def place(source, body):
        def step(i, carry):
            for s in range(8):
                bricks[s, i] = source[entry[s], i] * here[s]
            for s in range(8):
                rt, rl, rx = s // 4, (s // 2) % 2, s % 2
                for lx in range(2):
                    values = bricks[s, i, pl.ds(lx, 8, stride=2), :]
                    body(values, (rx * 2 + lx, rt * 8 + i, pl.ds(rl * 8, 8)))
            return carry
        lax.fori_loop(0, 8, step, 0)

    def emit(stage, x, t, values):
        tile = (
            2.0 * values
            + jnp.where(col == 0, 0.0, pltpu.roll(values, 1, 1))
            + jnp.where(col == 127, 0.0, pltpu.roll(values, 127, 1))
        )
        q_[stage][x + 1, t + 1] = tile
        es[stage][x, pl.ds(t, 1), :] = jnp.where(il == 0, tile[15:16], tile[0:1])

    def message(stage, which):
        dx, dt, dl = which
        i = MESSAGES.index(which)
        to = {"xt": ix + dx, "tb": it + dt, "luma": 1 - il if dl else il}
        if dl == 0:
            xs = {1: (4, 0), -1: (1, 5), 0: (pl.ds(1, 4), pl.ds(1, 4))}[dx]
            ts = {1: (16, 0), -1: (1, 17), 0: (pl.ds(1, 16), pl.ds(1, 16))}[dt]
            src, dst = (q_[stage].at[xs[j], ts[j]] for j in (0, 1))
        else:
            xs = {1: (3, 0), -1: (0, 5), 0: (pl.ds(0, 4), pl.ds(1, 4))}[dx]
            ts = {
                1: (pl.ds(8, 8), pl.ds(0, 8)),
                -1: (pl.ds(0, 8), pl.ds(24, 8)),
                0: (pl.ds(0, 16), pl.ds(8, 16)),
            }[dt]
            src, dst = es[stage].at[xs[0], ts[0]], er[stage].at[xs[1], ts[1]]
        return pltpu.make_async_remote_copy(
            src_ref=src, dst_ref=dst, send_sem=send_sem.at[stage, i], recv_sem=recv_sem.at[stage, i],
            device_id=to, device_id_type=MESH,
        )

    def guarded(which, sign, act):
        dx, dt, _ = which
        conds = []
        for d, at, size in ((dx * sign, ix, nx), (dt * sign, it, nt)):
            if d == 1:
                conds.append(at < size - 1)
            elif d == -1:
                conds.append(at > 0)
        if conds:
            pl.when(functools.reduce(jnp.logical_and, conds))(act)
        else:
            act()

    def send(stage, group):
        for which in group:
            guarded(which, 1, lambda which=which: message(stage, which).start())

    def receive(stage, group):
        for which in group:
            guarded(which, -1, lambda which=which: message(stage, which).wait_recv())

    def spread(stage, xs, update, carry):
        for x in xs:
            g = er[stage][x] + 2.0 * er[stage][x + 1] + er[stage][x + 2]
            fs[x] = g
            ff[x] = fs[x, pl.ds(7, 16)] + 2.0 * fs[x, pl.ds(8, 16)] + fs[x, pl.ds(9, 16)]
        need = sorted({x + d for x in xs for d in (0, 1, 2)})

        q = q_[stage]

        def step(i, carry):
            for t in (UNROLL * i + j for j in range(UNROLL)):
                sums = {x: q[x, t] + 2.0 * q[x, t + 1] + q[x, t + 2] for x in need}
                for x in xs:
                    a = sums[x] + 2.0 * sums[x + 1] + sums[x + 2]
                    smoothed = (
                        2.0 * a
                        + jnp.where(row == 0, 0.0, pltpu.roll(a, 1, 0))
                        + jnp.where(row == 15, 0.0, pltpu.roll(a, 15, 0))
                        + edge * ff[x, pl.ds(t, 1), :]
                    )
                    carry = update(x, t, smoothed, carry)
            return carry

        return lax.fori_loop(0, 16 // UNROLL, step, carry)

    def keep_sum(i, total):
        acc[pl.ds(i, 1), :] = jnp.sum(total, axis=0, keepdims=True)

    loads[0].wait()

    def put_n(values, at):
        n_[at] = values

    place(nin, put_n)

    def first(i, carry):
        for t in (UNROLL * i + j for j in range(UNROLL)):
            for x in range(4):
                emit(0, x, t, n_[x, t])
        return carry

    lax.fori_loop(0, 16 // UNROLL, first, 0)
    pl.semaphore_wait(barrier, peers - 1)
    send(0, SEND_ORDER)

    loads[1].wait()
    loads[2].wait()

    def put_c(values, at):
        c_[at] = values

    def put_r(values, at):
        r_[at] = c_[at] * values

    place(cin, put_c)
    place(tin, put_r)
    acc[...] = jnp.zeros((8, 128), jnp.float32)

    def update0(x, t, smoothed, carry):
        n = n_[x, t]
        diag = n * smoothed * (1.0 / 32.0) + c_[x, t]
        inverse = jnp.where(diag > 0.0, 1.0 / jnp.where(diag > 0.0, diag, 1.0), 0.0)
        r = r_[x, t]
        p = inverse * r
        d_[x, t] = diag
        m_[x, t] = inverse
        p0_[x, t] = p
        emit(1, x, t, n * p)
        return (carry[0] + r * p,)

    def image(p_ref, x, t, smoothed):
        p, n = p_ref[x, t], n_[x, t]
        return p, n, d_[x, t] * p - n * smoothed * (1.0 / 32.0)

    def update1(x, t, smoothed, carry):
        p, n, u = image(p0_, x, t, smoothed)
        later = m_[x, t] * u - SHIFT * p
        u0_[x, t] = u
        p1_[x, t] = later
        emit(2, x, t, n * later)
        return carry[0] + u * p, carry[1] + u * later

    def update2(x, t, smoothed, carry):
        p, n, u = image(p1_, x, t, smoothed)
        later = m_[x, t] * u - SHIFT * p
        p2_[x, t] = later
        emit(3, x, t, n * later)
        return carry[0] + u * p, carry[1] + u0_[x, t] * later, carry[2] + u * later

    def update3(x, t, smoothed, carry):
        p, n, u = image(p2_, x, t, smoothed)
        return (carry[0] + u * p,)

    rows = 0
    for stage, (update, count) in enumerate(((update0, 1), (update1, 2), (update2, 3), (update3, 1))):
        receive(stage, NEAR)
        carry = spread(stage, (1, 2), update, (zero,) * count)
        rest = SEND_ORDER
        for x, way in ((3, 1), (0, -1)) if stage % 2 else ((0, -1), (3, 1)):
            receive(stage, [m for m in FAR if m[0] == -way])
            carry = spread(stage, (x,), update, carry)
            if stage + 1 < STAGES:
                ready = [m for m in rest if m[0] == way or x == 3 * (1 - stage % 2)]
                send(stage + 1, ready)
                rest = [m for m in rest if m not in ready]
        for total in carry:
            keep_sum(rows, total)
            rows += 1

    each_peer(
        lambda r: pltpu.make_async_remote_copy(
            src_ref=acc, dst_ref=gathered.at[r - 1], send_sem=sum_send, recv_sem=sum_recv,
            device_id=peer_id(r), device_id_type=MESH,
        ).start()
    )
    pltpu.make_async_copy(gathered, gathered, sum_recv).wait()
    total = acc[...] + jnp.sum(gathered[...], axis=0)
    total = jnp.sum(total, axis=1, keepdims=True)
    b0, g00, g01, g11, g02, g12, g22 = (total[i : i + 1] for i in range(7))
    b1 = g00 - SHIFT * b0
    b2 = g01 - SHIFT * b1
    l10, l20 = g01 / g00, g02 / g00
    d1 = g11 - l10 * g01
    e12 = g12 - l20 * g01
    l21 = e12 / d1
    d2 = g22 - l20 * g02 - l21 * e12
    y1 = b1 - l10 * b0
    y2 = b2 - l20 * b0 - l21 * y1
    x2 = y2 / d2
    x1 = y1 / d1 - l21 * x2
    x0 = b0 / g00 - l10 * x1 - l20 * x2
    w0, w1, w2 = (jnp.broadcast_to(v, (8, 128)) for v in (x0, x1, x2))

    def combine(i, carry):
        for s in range(8):
            rt, rl, rx = s // 4, (s // 2) % 2, s % 2
            for lx in range(2):
                at = (rx * 2 + lx, rt * 8 + i, pl.ds(rl * 8, 8))
                bricks[s, i, pl.ds(lx, 8, stride=2), :] = w0 * p0_[at] + w1 * p1_[at] + w2 * p2_[at]
        for k in range(4):
            out[k, i] = bricks[slots[0, 0, 0, k], i] * kept[k]
        return carry

    kept = [jnp.where(k < counts[0, 0, 0], 1.0, 0.0) for k in range(4)]
    lax.fori_loop(0, 8, combine, 0)

    for stage in range(STAGES):
        for which in MESSAGES:
            guarded(which, 1, lambda which=which: message(stage, which).wait_send())
    pltpu.make_async_copy(gathered, gathered, sum_send).wait()


def per_device(nx, nt, target, confidence, normalizer, brick_slots, brick_counts):
    shape = (4, 8, 16, 128)
    whole = (4, 16, 16, 128)
    peers = nx * nt * 2
    vmem = lambda *dims: pltpu.VMEM(dims, jnp.float32)
    smem = pl.BlockSpec(memory_space=pltpu.SMEM)
    anywhere = pl.BlockSpec(memory_space=pl.ANY)
    out = pl.pallas_call(
        functools.partial(kernel, nx, nt),
        out_shape=jax.ShapeDtypeStruct(shape, jnp.float32),
        in_specs=[smem, smem, anywhere, anywhere, anywhere],
        out_specs=pl.BlockSpec(memory_space=pltpu.VMEM),
        scratch_shapes=[vmem(*shape)] * 3
        + [vmem(8, 8, 16, 128)]
        + [vmem(*whole)] * 9
        + [vmem(6, 18, 16, 128)] * STAGES
        + [vmem(4, 16, 128)] * STAGES
        + [vmem(6, 32, 128)] * STAGES
        + [
            vmem(4, 32, 128),
            vmem(4, 16, 128),
            vmem(8, 128),
            vmem(peers - 1, 8, 128),
            pltpu.SemaphoreType.DMA((3,)),
            pltpu.SemaphoreType.DMA((STAGES, len(MESSAGES))),
            pltpu.SemaphoreType.DMA((STAGES, len(MESSAGES))),
            pltpu.SemaphoreType.DMA,
            pltpu.SemaphoreType.DMA,
        ],
        compiler_params=pltpu.CompilerParams(
            collective_id=0, has_side_effects=True, vmem_limit_bytes=60 * 1024 * 1024
        ),
    )(
        brick_slots, brick_counts,
        target.reshape(shape), confidence.reshape(shape), normalizer.reshape(shape),
    )
    return out.reshape(target.shape)


def solution(mesh):
    split = P(("clip", "xt"), "tb", "luma", None, None, None, None, None)
    in_specs = (
        split,
        split,
        split,
        P(("clip", "xt"), "tb", "luma", None),
        P(("clip", "xt"), "tb", "luma"),
    )
    return jax.shard_map(
        functools.partial(per_device, mesh.shape["xt"], mesh.shape["tb"]),
        mesh=mesh, in_specs=in_specs, out_specs=split, check_vma=False,
    )
```
